32 devices in a mesh: ctx: 16 (over z, x, core), exp: 2 (over y).
Axes of the slice: x: 2, y: 2, z: 4, core: 2. Of those that a mesh axis runs over, the one named last changes fastest.
Arguments:
- hidden: bfloat16 [4096, 2048], P(('ctx', 'exp')), may hold values from -1.5 to 1.5
- lengths: int32 [2], replicated, may hold values from 1024 to 2048, as said below
- routes: int32 [4096, 8], P(('ctx', 'exp')), may hold values from 0 to 127, all different within a row; in each aligned block of 128 rows (0 to 127, 128 to 255, ...) at most 16 rows name the same one
- gates: float32 [4096, 8], P(('ctx', 'exp')), may hold values from 0.05 to 0.5
- attn_gain: float32 [2048], replicated, may hold values from 0.25 to 1.75
- q_weight: bfloat16 [2048, 4096], P('ctx', 'exp'), may hold values from -0.125 to 0.125
- key_value_weight: bfloat16 [2048, 1024], P('ctx'), may hold values from -0.125 to 0.125
- q_gain: float32 [128], replicated, may hold values from 0.25 to 1.75
- k_gain: float32 [128], replicated, may hold values from 0.25 to 1.75
- o_weight: bfloat16 [4096, 2048], P('exp', 'ctx'), may hold values from -0.09375 to 0.09375
- moe_gain: float32 [2048], replicated, may hold values from 0.25 to 1.75
- expert_in: bfloat16 [128, 2048, 1536], P(('ctx', 'exp')), may hold values from -0.125 to 0.125
- expert_out: bfloat16 [128, 768, 2048], P(('ctx', 'exp')), may hold values from -0.21875 to 0.21875
Outputs:
- new_hidden: bfloat16 [4096, 2048], P(('ctx', 'exp'))
- cache: bfloat16 [2, 4096, 512], P(None, 'ctx', 'exp')
The draws below stay inside these ranges and needn't reach their ends.
Inputs may be any that keep to these rules, and one draw needn't show every extreme that they name: `lengths`: one of the two prompts has exactly 2048 positions; the other has 1024 to 2048. `routes`: A row names 8 different experts. Within the 128 rows of each device (aligned blocks of rows) no expert is named more than 16 times, a bound that some block reaches.
All inputs are finite; a program needn't handle non-finite values.
Results may differ from the reference program's by a relative error of at most 0.02.
Values may be sent and summed in bfloat16 or wider, within the bound.
A program may use at most 128 MiB of HBM per device.

```python
import math
import jax
import jax.numpy as jnp
import numpy as np
from jax import lax

MODEL_WIDTH = 2048
QUERY_HEADS = 32
KEY_VALUE_HEADS = 4
HEAD_SIZE = 128
EXPERTS = 128
TOP = 8
FF = 768
TOK_CTX = 256
PACKED_LENGTH = 4096
LMAX = 2048
TOK_DEV = 128
SLICES = 1
FFS = 768
CAP = 16
N_CTX = 16
N_EXP = 2


def draw_lengths(key, part):
    picker = jax.random.randint(jax.random.fold_in(key, 11), (), 0, 2)
    shorter = jax.random.randint(jax.random.fold_in(key, 12), (), LMAX // 2, LMAX + 1)
    first_len = jnp.where(picker == 0, LMAX, shorter)
    second_len = jnp.where(picker == 0, shorter, LMAX)
    return jnp.stack([first_len, second_len]).astype(jnp.int32)


def levels(key, shape, split, low, high):
    level, own = 1.0, jax.random.fold_in(key, 6)
    for position, blocks in split:
        heights = jnp.exp(jax.random.uniform(jax.random.fold_in(own, position), (blocks,), jnp.float32, low / len(split), high / len(split)))
        level = level * jnp.repeat(heights, shape[position] // blocks).reshape([-1 if axis == position else 1 for axis in range(len(shape))])
    return level


def shared_out(rng, own, number, rows, count, top, reach, slope):
    order = jax.random.permutation(rng, count)
    crowded, ordinary = load_shares(count, rows * top, reach, slope, True), load_shares(count, rows * top, reach, slope, False)
    places = jnp.arange(count)

    def named(sizes, offset_by):
        used = int((sizes > 0).sum())
        fixed = max(1, used // 4)
        shifted = fixed + (places - fixed + offset_by * (used - fixed)) % max(1, count - fixed)
        return jnp.zeros((count,), jnp.int32).at[order[jnp.where(places < fixed, places, shifted)]].set(jnp.asarray(sizes, jnp.int32))

    sizes = jnp.where(number % 4 == 0, named(crowded, number // 4), named(ordinary, number - number // 4 - 1))
    mixed = jax.random.permutation(jax.random.fold_in(own, 3), count)
    giver, receiver = mixed[0:count // 2 * 2:2], mixed[1:count // 2 * 2:2]
    slack = jnp.minimum(sizes[giver] - 1, reach - sizes[receiver]) // 2
    slack = jnp.where((giver == order[0]) | (receiver == order[0]) | (sizes[receiver] == 0), 0, jnp.maximum(slack, 0))
    shifted = jax.random.randint(jax.random.fold_in(own, 4), (count // 2,), 0, 1 << 20) % (slack + 1)
    sizes = sizes.at[giver].add(-shifted).at[receiver].add(shifted)
    labels = jnp.searchsorted(jnp.cumsum(sizes), jnp.arange(rows * top), side="right").astype(jnp.int32)
    table = labels.reshape(top, rows).T
    table = table[jax.random.permutation(jax.random.fold_in(own, 1), rows)]
    offset_by = jax.random.randint(jax.random.fold_in(own, 2), (rows, 1), 0, top)
    return jnp.take_along_axis(table, (jnp.arange(top)[None, :] + offset_by) % top, axis=1)


def load_shares(amount, total, most, lean, full):
    portions = [(1 << 20) // math.isqrt(rank ** lean) + 1 for rank in range(1, amount + 1)]
    largest = most if full else min(most, max(-(-total // amount), total * portions[0] // sum(portions)))
    least = 1 if total - largest >= amount - 1 else 0
    given, rest = [largest] + [least] * (amount - 1), total - largest - least * (amount - 1)
    while rest > 0:
        movable = [i for i in range(1, amount) if given[i] < largest] or [i for i in range(1, amount) if given[i] < most]
        pool, budget = sum([portions[i] for i in movable]), rest
        for i in movable:
            extra = min(most - given[i], max(1, budget * portions[i] // pool), rest)
            given[i] = given[i] + extra
            rest = rest - extra
    return np.array(given)


def normal_values(key, dims, deviation, most, shards=(), kind=jnp.bfloat16):
    array = deviation * jax.random.normal(key, dims, jnp.float32)
    if shards:
        array = array * levels(key, dims, shards, -0.22, 0.18)
    return jnp.clip(array, -most, most).astype(kind)


def setup_inputs(seed: int = 0) -> dict:
    key_list = jax.random.split(jax.random.key(seed), 14)
    hidden = normal_values(key_list[0], (PACKED_LENGTH, MODEL_WIDTH), 0.25, 1.5, ((0, 32),))
    lengths = draw_lengths(jax.random.fold_in(key_list[13], 71), 0)
    routes_keys = jax.random.split(jax.random.fold_in(key_list[2], 1), PACKED_LENGTH // TOK_DEV)
    routes_turns = jax.random.permutation(jax.random.fold_in(key_list[2], 3), PACKED_LENGTH // TOK_DEV)
    routes = jax.vmap(lambda own, number: shared_out(jax.random.fold_in(key_list[2], 2), own, number, TOK_DEV, EXPERTS, TOP, CAP, 2))(routes_keys, routes_turns).reshape((PACKED_LENGTH, TOP))
    gates = jnp.clip(jnp.exp(math.log(0.5) - 2.3025851 * jax.random.uniform(key_list[3], (PACKED_LENGTH, TOP), jnp.float32) ** levels(key_list[3], (PACKED_LENGTH, TOP), ((0, 32),), -0.2, 0.2)), 0.05, 0.5)
    attn_gain = jnp.clip(1.0 + 0.15 * jax.random.normal(key_list[4], (MODEL_WIDTH,), jnp.float32), 0.25, 1.75)
    q_weight = normal_values(key_list[5], (MODEL_WIDTH, QUERY_HEADS * HEAD_SIZE), MODEL_WIDTH ** -0.5, 0.125, ((0, 16), (1, 2)))
    key_value_weight = normal_values(key_list[6], (MODEL_WIDTH, 2 * KEY_VALUE_HEADS * HEAD_SIZE), MODEL_WIDTH ** -0.5, 0.125, ((0, 16),))
    q_gain = jnp.clip(1.0 + 0.15 * jax.random.normal(key_list[7], (HEAD_SIZE,), jnp.float32), 0.25, 1.75)
    k_gain = jnp.clip(1.0 + 0.15 * jax.random.normal(key_list[8], (HEAD_SIZE,), jnp.float32), 0.25, 1.75)
    o_weight = normal_values(key_list[9], (QUERY_HEADS * HEAD_SIZE, MODEL_WIDTH), (QUERY_HEADS * HEAD_SIZE) ** -0.5, 0.09375, ((0, 2), (1, 16)))
    moe_gain = jnp.clip(1.0 + 0.15 * jax.random.normal(key_list[10], (MODEL_WIDTH,), jnp.float32), 0.25, 1.75)
    expert_in = normal_values(key_list[11], (EXPERTS * SLICES, MODEL_WIDTH, 2 * FFS), MODEL_WIDTH ** -0.5, 0.125, ((0, 32),))
    expert_out = normal_values(key_list[12], (EXPERTS * SLICES, FFS, MODEL_WIDTH), FF ** -0.5, 0.21875, ((0, 32),))
    return dict(hidden=hidden, lengths=lengths, routes=routes, gates=gates, attn_gain=attn_gain, q_weight=q_weight, key_value_weight=key_value_weight, q_gain=q_gain, k_gain=k_gain, o_weight=o_weight, moe_gain=moe_gain, expert_in=expert_in, expert_out=expert_out)


epsilon = 1e-06
rope_base = 1000000.0

def rms_scale(values, gain):
    mean_square = lax.optimization_barrier(jnp.mean(values * values, axis=-1, keepdims=True))
    return values * lax.rsqrt(mean_square + epsilon) * gain

def mirrored_position(row_ids, count_ctx, tok_ctx):
    half_rows = tok_ctx // 2
    holder = row_ids // tok_ctx
    within = row_ids % tok_ctx
    block_no = jnp.where(within < half_rows, holder, 2 * count_ctx - 1 - holder)
    return (block_no * half_rows + within % half_rows).astype(jnp.int32)

def document_info(token_positions, lengths):
    first_end = lengths[0]
    second_end = lengths[0] + lengths[1]
    document = (token_positions >= first_end).astype(jnp.int32) + (token_positions >= second_end).astype(jnp.int32)
    doc_start = jnp.where(document == 0, 0, jnp.where(document == 1, first_end, second_end))
    return (document, (token_positions - doc_start).astype(jnp.int32))

def rotate(values, rope_pos):
    head_width = values.shape[-1]
    freq_ids = jnp.arange(head_width // 2, dtype=jnp.float32)
    inverse = rope_base ** (-2.0 * freq_ids / head_width)
    angles = rope_pos.astype(jnp.float32)[:, None] * inverse[None, :]
    cosine = jnp.cos(angles)[:, None, :]
    sine_part = jnp.sin(angles)[:, None, :]
    first_half = values[..., :head_width // 2]
    second_half = values[..., head_width // 2:]
    return jnp.concatenate([first_half * cosine - second_half * sine_part, second_half * cosine + first_half * sine_part], axis=-1)

def reference(hidden, lengths, routes, gates, attn_gain, q_weight, key_value_weight, q_gain, k_gain, o_weight, moe_gain, expert_in, expert_out):
    row_ids = jnp.arange(PACKED_LENGTH, dtype=jnp.int32)
    token_positions = mirrored_position(row_ids, N_CTX, TOK_CTX)
    document, rope_pos = document_info(token_positions, lengths)
    normed = rms_scale(hidden.astype(jnp.float32), attn_gain).astype(jnp.bfloat16)
    q_raw = jnp.dot(normed, q_weight, preferred_element_type=jnp.float32).reshape(PACKED_LENGTH, QUERY_HEADS, HEAD_SIZE)
    key_value_plain = jnp.dot(normed, key_value_weight, preferred_element_type=jnp.float32)
    key_unrotated = key_value_plain[:, :KEY_VALUE_HEADS * HEAD_SIZE].reshape(PACKED_LENGTH, KEY_VALUE_HEADS, HEAD_SIZE)
    queries = rotate(rms_scale(q_raw, q_gain), rope_pos).astype(jnp.bfloat16)
    key_row_block = rotate(rms_scale(key_unrotated, k_gain), rope_pos).astype(jnp.bfloat16)
    value_row_block = key_value_plain[:, KEY_VALUE_HEADS * HEAD_SIZE:].astype(jnp.bfloat16).reshape(PACKED_LENGTH, KEY_VALUE_HEADS, HEAD_SIZE)
    head_groups = QUERY_HEADS // KEY_VALUE_HEADS
    score_scale = HEAD_SIZE ** (-0.5)
    allowed = (document[:, None] == document[None, :]) & (token_positions[None, :] <= token_positions[:, None])

    def one_head(head_id):
        query = lax.dynamic_index_in_dim(queries, head_id, 1, keepdims=False)
        key_head = lax.dynamic_index_in_dim(key_row_block, head_id // head_groups, 1, keepdims=False)
        value_head = lax.dynamic_index_in_dim(value_row_block, head_id // head_groups, 1, keepdims=False)
        scores = jnp.dot(query, key_head.T, preferred_element_type=jnp.float32) * score_scale
        weights = jnp.where(allowed, jnp.exp(scores), 0.0).astype(jnp.bfloat16)
        totals = lax.optimization_barrier(jnp.sum(weights.astype(jnp.float32), axis=1))
        context = jnp.dot(weights, value_head, preferred_element_type=jnp.float32) / totals[:, None]
        return context.astype(jnp.bfloat16)
    contexts = lax.map(one_head, jnp.arange(QUERY_HEADS, dtype=jnp.int32))
    context_rows = jnp.transpose(contexts, (1, 0, 2)).reshape(PACKED_LENGTH, QUERY_HEADS * HEAD_SIZE)
    residual_mid = hidden.astype(jnp.float32) + jnp.dot(context_rows, o_weight, preferred_element_type=jnp.float32)
    moe_in = rms_scale(residual_mid, moe_gain).astype(jnp.bfloat16)
    inner = expert_in.reshape(EXPERTS, SLICES, MODEL_WIDTH, 2 * FFS)
    outer = expert_out.reshape(EXPERTS, SLICES, FFS, MODEL_WIDTH)
    most_rows = N_CTX * N_EXP * CAP

    def one_expert(moe_sum, expert_id):
        hits = routes == expert_id
        weight_row = lax.optimization_barrier(jnp.sum(jnp.where(hits, gates, 0.0), axis=1))
        chosen = jnp.any(hits, axis=1)
        index_rows = jnp.nonzero(chosen, size=most_rows, fill_value=0)[0].astype(jnp.int32)
        valid = (jnp.arange(most_rows, dtype=jnp.int32) < jnp.sum(chosen.astype(jnp.int32))).astype(jnp.float32)
        taken = moe_in[index_rows]
        w_inner = lax.dynamic_index_in_dim(inner, expert_id, 0, keepdims=False)
        w_outer = lax.dynamic_index_in_dim(outer, expert_id, 0, keepdims=False)
        gate_up = jnp.einsum('rd,sdf->srf', taken.astype(jnp.float32), w_inner.astype(jnp.float32))
        activated = (jax.nn.silu(gate_up[..., :FFS]) * gate_up[..., FFS:]).astype(jnp.bfloat16)
        produced = jnp.einsum('srf,sfd->srd', activated.astype(jnp.float32), w_outer.astype(jnp.float32)).astype(jnp.bfloat16)
        summed = lax.optimization_barrier(jnp.sum(produced.astype(jnp.float32), axis=0))
        contrib = summed * (weight_row[index_rows] * valid)[:, None]
        return (moe_sum.at[index_rows].add(contrib), None)
    moe_out, unused_tail = lax.scan(one_expert, jnp.zeros((PACKED_LENGTH, MODEL_WIDTH), jnp.float32), jnp.arange(EXPERTS, dtype=jnp.int32))
    new_hidden = (residual_mid + moe_out).astype(jnp.bfloat16)
    key_store_cache = jnp.zeros((PACKED_LENGTH, KEY_VALUE_HEADS * HEAD_SIZE), jnp.bfloat16).at[token_positions].set(key_row_block.reshape(PACKED_LENGTH, KEY_VALUE_HEADS * HEAD_SIZE))
    value_store_cache = jnp.zeros((PACKED_LENGTH, KEY_VALUE_HEADS * HEAD_SIZE), jnp.bfloat16).at[token_positions].set(value_row_block.reshape(PACKED_LENGTH, KEY_VALUE_HEADS * HEAD_SIZE))
    return (new_hidden, jnp.stack([key_store_cache, value_store_cache]))
```

```python
import functools
import jax
import jax.numpy as jnp
from jax import lax
from jax.experimental import pallas as pl
from jax.experimental.pallas import tpu as pltpu
from jax.sharding import PartitionSpec as P

MODEL_WIDTH = 2048
QUERY_HEADS = 32
KEY_VALUE_HEADS = 4
HEAD_SIZE = 128
EXPERTS = 128
TOP = 8


epsilon = 1e-06
rope_base = 1000000.0


def rms_scale(values, gain):
    mean_square = jnp.mean(values * values, axis=-1, keepdims=True)
    return values * lax.rsqrt(mean_square + epsilon) * gain


def mirrored_position(row_ids, count_ctx, tok_ctx):
    half_rows = tok_ctx // 2
    holder = row_ids // tok_ctx
    within = row_ids % tok_ctx
    block_no = jnp.where(within < half_rows, holder, 2 * count_ctx - 1 - holder)
    return block_no * half_rows + within % half_rows


def document_info(token_positions, lengths):
    first_end = lengths[0]
    second_end = lengths[0] + lengths[1]
    document = (token_positions >= first_end).astype(jnp.int32) + (
        token_positions >= second_end
    ).astype(jnp.int32)
    doc_start = jnp.where(document == 0, 0, jnp.where(document == 1, first_end, second_end))
    return (document, token_positions - doc_start)


def rotate(values, rope_pos):
    head_width = values.shape[-1]
    freq_ids = jnp.arange(head_width // 2, dtype=jnp.float32)
    inverse = rope_base ** (-2.0 * freq_ids / head_width)
    angles = rope_pos.astype(jnp.float32)[:, None] * inverse[None, :]
    cosine = jnp.cos(angles)[:, None, :]
    sine_part = jnp.sin(angles)[:, None, :]
    first_half = values[..., : head_width // 2]
    second_half = values[..., head_width // 2 :]
    return jnp.concatenate(
        [
            first_half * cosine - second_half * sine_part,
            second_half * cosine + first_half * sine_part,
        ],
        axis=-1,
    )


MESH = pl.DeviceIdType.MESH
CHUNKS = 4
KEY_TILE = 256


def attention_kernel(count_ctx, half_rows, group, len_ref, q_ref, k_ref, v_ref, o_ref, q_all, total):
    my_ctx = lax.axis_index("ctx")
    first_end = len_ref[0]
    second_end = len_ref[0] + len_ref[1]
    score_scale = HEAD_SIZE ** (-0.5)
    ones = jnp.ones((KEY_TILE, HEAD_SIZE), jnp.bfloat16)

    def doc_of(pos):
        return (pos >= first_end).astype(jnp.int32) + (pos >= second_end).astype(jnp.int32)

    for half in range(2):
        block_no = my_ctx if half == 0 else 2 * count_ctx - 1 - my_ctx
        start = block_no * half_rows
        rows = pl.ds(half * half_rows, half_rows)
        for head in range(group):
            q_all[pl.ds(head * half_rows, half_rows), :] = q_ref[
                rows, pl.ds(head * HEAD_SIZE, HEAD_SIZE)
            ]
        total[...] = jnp.zeros_like(total)
        doc_start = jnp.where(
            start >= second_end, second_end, jnp.where(start >= first_end, first_end, 0)
        )
        query_pos = start + lax.broadcasted_iota(jnp.int32, (half_rows, KEY_TILE), 0)
        query_doc = doc_of(query_pos)

        def tile(index, carry):
            keys = k_ref[pl.ds(pl.multiple_of(index * KEY_TILE, KEY_TILE), KEY_TILE), :]
            values = v_ref[pl.ds(pl.multiple_of(index * KEY_TILE, KEY_TILE), KEY_TILE), :]
            key_pos = index * KEY_TILE + lax.broadcasted_iota(
                jnp.int32, (half_rows, KEY_TILE), 1
            )
            allowed = (doc_of(key_pos) == query_doc) & (key_pos <= query_pos)
            scores = lax.dot_general(
                q_all[...], keys, (((1,), (1,)), ((), ())), preferred_element_type=jnp.float32
            )
            scores = (scores * score_scale).reshape(group, half_rows, KEY_TILE)
            weights = jnp.where(allowed[None], jnp.exp(scores), 0.0).astype(jnp.bfloat16)
            total[...] += jnp.dot(
                weights.reshape(group * half_rows, KEY_TILE),
                jnp.concatenate([values, ones], axis=1),
                preferred_element_type=jnp.float32,
            )
            return carry

        lax.fori_loop(
            doc_start // KEY_TILE, (start + half_rows - 1) // KEY_TILE + 1, tile, 0
        )
        result = (total[:, :HEAD_SIZE] / total[:, HEAD_SIZE:]).astype(jnp.bfloat16)
        for head in range(group):
            o_ref[rows, pl.ds(head * HEAD_SIZE, HEAD_SIZE)] = result[
                head * half_rows : (head + 1) * half_rows
            ]


def attention(lengths, queries, keys, values, count_ctx, half_rows, share, group):
    length = keys.shape[0]
    width = group * HEAD_SIZE
    return pl.pallas_call(
        functools.partial(attention_kernel, count_ctx, half_rows, group),
        grid=(share,),
        in_specs=[
            pl.BlockSpec(memory_space=pltpu.SMEM),
            pl.BlockSpec((2 * half_rows, width), lambda i: (0, i)),
            pl.BlockSpec((length, HEAD_SIZE), lambda i: (0, i)),
            pl.BlockSpec((length, HEAD_SIZE), lambda i: (0, i)),
        ],
        out_specs=pl.BlockSpec((2 * half_rows, width), lambda i: (0, i)),
        out_shape=jax.ShapeDtypeStruct((2 * half_rows, share * width), jnp.bfloat16),
        scratch_shapes=[
            pltpu.VMEM((group * half_rows, HEAD_SIZE), jnp.bfloat16),
            pltpu.VMEM((group * half_rows, 2 * HEAD_SIZE), jnp.float32),
        ],
        compiler_params=pltpu.CompilerParams(vmem_limit_bytes=40 * 1024 * 1024),
        name="attention",
    )(lengths, queries, keys, values)


def reduce_kernel(
    Z, E, p_ref, o_ref, held, from_core, from_e, from_x, from_z, load_sem, send_sem, recv_sem
):
    ctx = lax.axis_index("ctx")
    e = lax.axis_index("exp")
    core = lax.rem(ctx, 2)
    x = lax.rem(ctx // 2, 2)
    z = ctx // 4
    width = held.shape[-1]
    sibling = (ctx + 1 - 2 * core, e)
    x_peer = (ctx + 2 - 4 * x, e)
    e_peer = [(ctx, lax.rem(e + d, E)) for d in range(1, E)]
    z_peer = [(lax.rem(z + d, Z) * 4 + lax.rem(ctx, 4), e) for d in range(1, Z)]
    z_next = [lax.rem(z + d, Z) for d in range(1, Z)]
    e_next = [lax.rem(e + d, E) for d in range(1, E)]

    barrier = pltpu.get_barrier_semaphore()
    peers = [sibling, x_peer] + e_peer + z_peer
    for peer in peers:
        pl.semaphore_signal(barrier, inc=1, device_id=peer, device_id_type=MESH)
    pl.semaphore_wait(barrier, len(peers))

    def remote(src, dst, k, slot, peer):
        copy = pltpu.make_async_remote_copy(
            src_ref=src,
            dst_ref=dst,
            send_sem=send_sem.at[k, slot],
            recv_sem=recv_sem.at[k, slot],
            device_id=peer,
            device_id_type=MESH,
        )
        copy.start()
        return copy

    def add(target, sources):
        value = target[...].astype(jnp.float32)
        for source in sources:
            value = value + source[...].astype(jnp.float32)
        target[...] = value.astype(jnp.bfloat16)

    first, local = [], []
    for k in range(CHUNKS):
        columns = pl.ds(k * width, width)
        first.append(
            remote(p_ref.at[:, :, 1 - core, :, :, columns], from_core.at[k], k, 0, sibling)
        )
        copy = pltpu.make_async_copy(
            p_ref.at[:, :, core, :, :, columns], held.at[k], load_sem.at[k]
        )
        copy.start()
        local.append(copy)

    def send_e(k, x_first):
        out = []
        for d in range(1, E):
            if x_first:
                src = held.at[k, :, x, e_next[d - 1]]
                dst = from_e.at[k, d - 1, :, 0]
            else:
                src = held.at[k, :, :, e_next[d - 1]]
                dst = from_e.at[k, d - 1]
            out.append(remote(src, dst, k, d, e_peer[d - 1]))
        return out

    def send_x(k, x_first):
        if x_first:
            return [remote(held.at[k, :, 1 - x], from_x.at[k], k, E, x_peer)]
        return [remote(held.at[k, :, 1 - x, e], from_x.at[k, :, 0], k, E, x_peer)]

    def add_e(k, x_first):
        @pl.loop(0, Z)
        def _(i):
            if x_first:
                add(held.at[k, i, x, e], [from_e.at[k, d, i, 0] for d in range(E - 1)])
            else:
                for j in range(2):
                    add(held.at[k, i, j, e], [from_e.at[k, d, i, j] for d in range(E - 1)])

    def add_x(k, x_first):
        @pl.loop(0, Z)
        def _(i):
            if x_first:

                @pl.loop(0, E)
                def _(j):
                    add(held.at[k, i, x, j], [from_x.at[k, i, j]])

            else:
                add(held.at[k, i, x, e], [from_x.at[k, i, 0]])

    flying = []
    sent = []
    for k in range(CHUNKS):
        local[k].wait()
        first[k].wait_recv()

        @pl.loop(0, Z)
        def _(i):
            @pl.loop(0, E)
            def _(j):
                for m in range(2):
                    add(held.at[k, i, m, j], [from_core.at[k, i, m, j]])

        flying.append(send_x(k, True) if k % 2 else send_e(k, False))
    sent += first
    for k in range(CHUNKS):
        for copy in flying[k]:
            copy.wait_recv()
        sent += flying[k]
        if k % 2:
            add_x(k, True)
            flying[k] = send_e(k, True)
        else:
            add_e(k, False)
            flying[k] = send_x(k, False)
    for k in range(CHUNKS):
        for copy in flying[k]:
            copy.wait_recv()
        sent += flying[k]
        if k % 2:
            add_e(k, True)
        else:
            add_x(k, False)
        flying[k] = [
            remote(held.at[k, z_next[d - 1], x, e], from_z.at[k, d - 1], k, E + d, z_peer[d - 1])
            for d in range(1, Z)
        ]
    for k in range(CHUNKS):
        for copy in flying[k]:
            copy.wait_recv()
        sent += flying[k]
        value = held[k, z, x, e].astype(jnp.float32)
        for d in range(Z - 1):
            value = value + from_z[k, d].astype(jnp.float32)
        o_ref[:, k * width : (k + 1) * width] = value
    for copy in sent:
        copy.wait_send()


def reduce_over_devices(partial, count_ctx, expert_count, tok_dev):
    Z = count_ctx // 4
    E = expert_count
    width = MODEL_WIDTH // CHUNKS
    slots = E + Z
    return pl.pallas_call(
        functools.partial(reduce_kernel, Z, E),
        in_specs=[pl.BlockSpec(memory_space=pl.ANY)],
        out_specs=pl.BlockSpec(memory_space=pltpu.VMEM),
        out_shape=jax.ShapeDtypeStruct((tok_dev, MODEL_WIDTH), jnp.float32),
        scratch_shapes=[
            pltpu.VMEM((CHUNKS, Z, 2, E, tok_dev, width), jnp.bfloat16),
            pltpu.VMEM((CHUNKS, Z, 2, E, tok_dev, width), jnp.bfloat16),
            pltpu.VMEM((CHUNKS, E - 1, Z, 2, tok_dev, width), jnp.bfloat16),
            pltpu.VMEM((CHUNKS, Z, E, tok_dev, width), jnp.bfloat16),
            pltpu.VMEM((CHUNKS, Z - 1, tok_dev, width), jnp.bfloat16),
            pltpu.SemaphoreType.DMA((CHUNKS,)),
            pltpu.SemaphoreType.DMA((CHUNKS, slots)),
            pltpu.SemaphoreType.DMA((CHUNKS, slots)),
        ],
        compiler_params=pltpu.CompilerParams(
            collective_id=0, has_side_effects=True, vmem_limit_bytes=VMEM_LIMIT
        ),
        name="reduce_over_devices",
    )(partial.reshape(Z, 2, 2, E, tok_dev, MODEL_WIDTH))


VMEM_LIMIT = 60 * 1024 * 1024


def shards(
    hidden,
    lengths,
    routes,
    gates,
    attn_gain,
    q_weight,
    key_value_weight,
    q_gain,
    k_gain,
    o_weight,
    moe_gain,
    expert_in,
    expert_out,
):
    count_ctx = lax.axis_size("ctx")
    expert_count = lax.axis_size("exp")
    my_ctx = lax.axis_index("ctx")
    my_exp = lax.axis_index("exp")
    tok_dev = hidden.shape[0]
    tok_ctx = tok_dev * expert_count
    half_rows = tok_ctx // 2
    head_groups = QUERY_HEADS // KEY_VALUE_HEADS
    q_dev = QUERY_HEADS // expert_count
    key_value_share = max(1, KEY_VALUE_HEADS // expert_count)
    group_dev = q_dev // key_value_share
    column_share = KEY_VALUE_HEADS * HEAD_SIZE // expert_count
    key_value_leading = my_exp * q_dev // head_groups
    col_offset = my_exp * column_share - key_value_leading * HEAD_SIZE
    query_pos = mirrored_position(
        my_ctx * tok_ctx + jnp.arange(tok_ctx, dtype=jnp.int32), count_ctx, tok_ctx
    )
    query_doc, query_rope = document_info(query_pos, lengths)
    normed_own = rms_scale(hidden.astype(jnp.float32), attn_gain).astype(jnp.bfloat16)
    normed = lax.all_gather(normed_own, "exp", axis=0, tiled=True)
    key_cols = lax.dynamic_slice_in_dim(
        key_value_weight, key_value_leading * HEAD_SIZE, key_value_share * HEAD_SIZE, 1
    )
    value_column_block = lax.dynamic_slice_in_dim(
        key_value_weight,
        KEY_VALUE_HEADS * HEAD_SIZE + key_value_leading * HEAD_SIZE,
        key_value_share * HEAD_SIZE,
        1,
    )
    kv_local = jnp.concatenate([key_cols, value_column_block], axis=1)
    q_raw = jnp.dot(
        normed,
        lax.all_gather(q_weight, "ctx", axis=0, tiled=True),
        preferred_element_type=jnp.float32,
    )
    key_value_plain = jnp.dot(
        normed,
        lax.all_gather(kv_local, "ctx", axis=0, tiled=True),
        preferred_element_type=jnp.float32,
    )
    queries = rotate(
        rms_scale(q_raw.reshape(tok_ctx, q_dev, HEAD_SIZE), q_gain), query_rope
    ).astype(jnp.bfloat16)
    key_row_block = rotate(
        rms_scale(
            key_value_plain[:, : key_value_share * HEAD_SIZE].reshape(
                tok_ctx, key_value_share, HEAD_SIZE
            ),
            k_gain,
        ),
        query_rope,
    ).astype(jnp.bfloat16)
    value_row_block = key_value_plain[:, key_value_share * HEAD_SIZE :].astype(jnp.bfloat16)
    key_values = jnp.stack(
        [key_row_block.reshape(tok_ctx, key_value_share * HEAD_SIZE), value_row_block]
    )
    gathered = lax.all_gather(key_values, "ctx", axis=0)
    ordered = jnp.concatenate(
        [
            jnp.moveaxis(gathered[:, :, :half_rows], 0, 1),
            jnp.moveaxis(gathered[::-1, :, half_rows:], 0, 1),
        ],
        axis=1,
    ).reshape(2, count_ctx * tok_ctx, key_value_share * HEAD_SIZE)
    cache = lax.dynamic_slice(
        ordered, (0, my_ctx * tok_ctx, col_offset), (2, tok_ctx, column_share)
    )
    context = attention(
        lengths,
        queries.reshape(tok_ctx, q_dev * HEAD_SIZE),
        ordered[0],
        ordered[1],
        count_ctx,
        half_rows,
        key_value_share,
        group_dev,
    )
    o_rows = lax.all_gather(o_weight.T, "ctx", axis=0, tiled=True)
    attn_part = lax.dot_general(
        context, o_rows, (((1,), (1,)), ((), ())), preferred_element_type=jnp.float32
    )
    attn_parts = attn_part.reshape(expert_count, tok_dev, MODEL_WIDTH)
    attn_own = lax.dynamic_index_in_dim(attn_parts, my_exp, 0, keepdims=False)
    for shift in range(1, expert_count):
        outgoing = lax.dynamic_index_in_dim(
            attn_parts, (my_exp + shift) % expert_count, 0, keepdims=False
        ).astype(jnp.bfloat16)
        route = [(i, (i + shift) % expert_count) for i in range(expert_count)]
        attn_own = attn_own + lax.ppermute(outgoing, "exp", route).astype(jnp.float32)
    residual_mid = hidden.astype(jnp.float32) + attn_own
    moe_in = rms_scale(residual_mid, moe_gain).astype(jnp.bfloat16)
    devices = count_ctx * expert_count
    slices = max(1, devices // EXPERTS)
    rows_dev = expert_in.shape[0]
    ffs_dev = expert_out.shape[1]
    capacity = max(4, 2 * tok_dev * TOP // EXPERTS)
    tokens = lax.all_gather(moe_in, ("ctx", "exp"), axis=0)
    table = lax.all_gather(
        jnp.concatenate([routes.astype(jnp.float32), gates], axis=1), ("ctx", "exp"), axis=0
    )
    my_device = my_ctx * expert_count + my_exp
    my_experts = (my_device * rows_dev + jnp.arange(rows_dev, dtype=jnp.int32)) // slices
    chosen = (
        table[:, None, :, :TOP].astype(jnp.int32) == my_experts[None, :, None, None]
    )
    hit = jnp.any(chosen, axis=3)
    token_gate = jnp.sum(jnp.where(chosen, table[:, None, :, TOP:], 0.0), axis=3)
    before = jnp.triu(jnp.ones((tok_dev, tok_dev), jnp.bfloat16), 1)
    ranking = jnp.einsum(
        "ait,tu->aiu", hit.astype(jnp.bfloat16), before, preferred_element_type=jnp.float32
    ).astype(jnp.int32)
    placed = hit[:, :, None, :] & (
        ranking[:, :, None, :] == jnp.arange(capacity, dtype=jnp.int32)[None, None, :, None]
    )
    slot_gate = jnp.sum(jnp.where(placed, token_gate[:, :, None, :], 0.0), axis=3)
    placement = placed.astype(jnp.bfloat16).reshape(devices, rows_dev * capacity, tok_dev)
    arrived = (
        jnp.einsum("ast,atd->asd", placement, tokens, preferred_element_type=jnp.float32)
        .astype(jnp.bfloat16)
        .reshape(devices, rows_dev, capacity, MODEL_WIDTH)
    )
    gate_up = jnp.einsum("arcd,rdf->arcf", arrived, expert_in, preferred_element_type=jnp.float32)
    activated = (
        jax.nn.silu(gate_up[..., :ffs_dev]) * gate_up[..., ffs_dev:] * slot_gate[..., None]
    ).astype(jnp.bfloat16)
    produced = jnp.einsum(
        "arcf,rfd->arcd", activated, expert_out, preferred_element_type=jnp.float32
    ).astype(jnp.bfloat16)
    partial = jnp.einsum(
        "ast,asd->atd",
        placement,
        produced.reshape(devices, rows_dev * capacity, MODEL_WIDTH),
        preferred_element_type=jnp.float32,
    ).astype(jnp.bfloat16)
    moe_out = reduce_over_devices(partial, count_ctx, expert_count, tok_dev)
    new_hidden = (residual_mid + moe_out).astype(jnp.bfloat16)
    return (new_hidden, cache)


def solution(mesh):
    in_specs = (
        P(("ctx", "exp"), None),
        P(),
        P(("ctx", "exp"), None),
        P(("ctx", "exp"), None),
        P(),
        P("ctx", "exp"),
        P("ctx", None),
        P(),
        P(),
        P("exp", "ctx"),
        P(),
        P(("ctx", "exp"), None, None),
        P(("ctx", "exp"), None, None),
    )
    out_specs = (P(("ctx", "exp"), None), P(None, "ctx", "exp"))
    return jax.shard_map(shards, mesh=mesh, in_specs=in_specs, out_specs=out_specs, check_vma=False)
```

```python
import functools
import jax
import jax.numpy as jnp
from jax import lax
from jax.experimental import pallas as pl
from jax.experimental.pallas import tpu as pltpu
from jax.sharding import PartitionSpec as P

MODEL_WIDTH = 2048
QUERY_HEADS = 32
KEY_VALUE_HEADS = 4
HEAD_SIZE = 128
EXPERTS = 128
TOP = 8


epsilon = 1e-06
rope_base = 1000000.0


def rms_scale(values, gain):
    mean_square = jnp.mean(values * values, axis=-1, keepdims=True)
    return values * lax.rsqrt(mean_square + epsilon) * gain


def mirrored_position(row_ids, count_ctx, tok_ctx):
    half_rows = tok_ctx // 2
    holder = row_ids // tok_ctx
    within = row_ids % tok_ctx
    block_no = jnp.where(within < half_rows, holder, 2 * count_ctx - 1 - holder)
    return block_no * half_rows + within % half_rows


def document_info(token_positions, lengths):
    first_end = lengths[0]
    second_end = lengths[0] + lengths[1]
    document = (token_positions >= first_end).astype(jnp.int32) + (
        token_positions >= second_end
    ).astype(jnp.int32)
    doc_start = jnp.where(document == 0, 0, jnp.where(document == 1, first_end, second_end))
    return (document, token_positions - doc_start)


def rotate(values, rope_pos):
    head_width = values.shape[-1]
    freq_ids = jnp.arange(head_width // 2, dtype=jnp.float32)
    inverse = rope_base ** (-2.0 * freq_ids / head_width)
    angles = rope_pos.astype(jnp.float32)[:, None] * inverse[None, :]
    cosine = jnp.cos(angles)[:, None, :]
    sine_part = jnp.sin(angles)[:, None, :]
    first_half = values[..., : head_width // 2]
    second_half = values[..., head_width // 2 :]
    return jnp.concatenate(
        [
            first_half * cosine - second_half * sine_part,
            second_half * cosine + first_half * sine_part,
        ],
        axis=-1,
    )


MESH = pl.DeviceIdType.MESH
CHUNKS = 4
KEY_TILE = 256


def attention_kernel(count_ctx, half_rows, group, len_ref, q_ref, k_ref, v_ref, o_ref, q_all, total):
    my_ctx = lax.axis_index("ctx")
    first_end = len_ref[0]
    second_end = len_ref[0] + len_ref[1]
    score_scale = HEAD_SIZE ** (-0.5)
    ones = jnp.ones((KEY_TILE, HEAD_SIZE), jnp.bfloat16)

    def doc_of(pos):
        return (pos >= first_end).astype(jnp.int32) + (pos >= second_end).astype(jnp.int32)

    for half in range(2):
        block_no = my_ctx if half == 0 else 2 * count_ctx - 1 - my_ctx
        start = block_no * half_rows
        rows = pl.ds(half * half_rows, half_rows)
        for head in range(group):
            q_all[pl.ds(head * half_rows, half_rows), :] = q_ref[
                rows, pl.ds(head * HEAD_SIZE, HEAD_SIZE)
            ]
        total[...] = jnp.zeros_like(total)
        doc_start = jnp.where(
            start >= second_end, second_end, jnp.where(start >= first_end, first_end, 0)
        )
        query_pos = start + lax.broadcasted_iota(jnp.int32, (half_rows, KEY_TILE), 0)
        query_doc = doc_of(query_pos)

        def tile(index, carry):
            keys = k_ref[pl.ds(pl.multiple_of(index * KEY_TILE, KEY_TILE), KEY_TILE), :]
            values = v_ref[pl.ds(pl.multiple_of(index * KEY_TILE, KEY_TILE), KEY_TILE), :]
            key_pos = index * KEY_TILE + lax.broadcasted_iota(
                jnp.int32, (half_rows, KEY_TILE), 1
            )
            allowed = (doc_of(key_pos) == query_doc) & (key_pos <= query_pos)
            scores = lax.dot_general(
                q_all[...], keys, (((1,), (1,)), ((), ())), preferred_element_type=jnp.float32
            )
            scores = (scores * score_scale).reshape(group, half_rows, KEY_TILE)
            weights = jnp.where(allowed[None], jnp.exp(scores), 0.0).astype(jnp.bfloat16)
            total[...] += jnp.dot(
                weights.reshape(group * half_rows, KEY_TILE),
                jnp.concatenate([values, ones], axis=1),
                preferred_element_type=jnp.float32,
            )
            return carry

        lax.fori_loop(
            doc_start // KEY_TILE, (start + half_rows - 1) // KEY_TILE + 1, tile, 0
        )
        result = (total[:, :HEAD_SIZE] / total[:, HEAD_SIZE:]).astype(jnp.bfloat16)
        for head in range(group):
            o_ref[rows, pl.ds(head * HEAD_SIZE, HEAD_SIZE)] = result[
                head * half_rows : (head + 1) * half_rows
            ]


def attention(lengths, queries, keys, values, count_ctx, half_rows, share, group):
    length = keys.shape[0]
    width = group * HEAD_SIZE
    return pl.pallas_call(
        functools.partial(attention_kernel, count_ctx, half_rows, group),
        grid=(share,),
        in_specs=[
            pl.BlockSpec(memory_space=pltpu.SMEM),
            pl.BlockSpec((2 * half_rows, width), lambda i: (0, i)),
            pl.BlockSpec((length, HEAD_SIZE), lambda i: (0, i)),
            pl.BlockSpec((length, HEAD_SIZE), lambda i: (0, i)),
        ],
        out_specs=pl.BlockSpec((2 * half_rows, width), lambda i: (0, i)),
        out_shape=jax.ShapeDtypeStruct((2 * half_rows, share * width), jnp.bfloat16),
        scratch_shapes=[
            pltpu.VMEM((group * half_rows, HEAD_SIZE), jnp.bfloat16),
            pltpu.VMEM((group * half_rows, 2 * HEAD_SIZE), jnp.float32),
        ],
        compiler_params=pltpu.CompilerParams(vmem_limit_bytes=40 * 1024 * 1024),
        name="attention",
    )(lengths, queries, keys, values)


def reduce_kernel(
    Z, E, p_ref, o_ref, held, from_core, from_e, from_x, from_z, load_sem, send_sem, recv_sem
):
    ctx = lax.axis_index("ctx")
    e = lax.axis_index("exp")
    core = lax.rem(ctx, 2)
    x = lax.rem(ctx // 2, 2)
    z = ctx // 4
    width = held.shape[-1]
    sibling = (ctx + 1 - 2 * core, e)
    x_peer = (ctx + 2 - 4 * x, e)
    e_peer = [(ctx, lax.rem(e + d, E)) for d in range(1, E)]
    z_peer = [(lax.rem(z + d, Z) * 4 + lax.rem(ctx, 4), e) for d in range(1, Z)]
    z_next = [lax.rem(z + d, Z) for d in range(1, Z)]
    e_next = [lax.rem(e + d, E) for d in range(1, E)]

    barrier = pltpu.get_barrier_semaphore()
    peers = [sibling, x_peer] + e_peer + z_peer
    for peer in peers:
        pl.semaphore_signal(barrier, inc=1, device_id=peer, device_id_type=MESH)
    pl.semaphore_wait(barrier, len(peers))

    def remote(src, dst, k, slot, peer):
        copy = pltpu.make_async_remote_copy(
            src_ref=src,
            dst_ref=dst,
            send_sem=send_sem.at[k, slot],
            recv_sem=recv_sem.at[k, slot],
            device_id=peer,
            device_id_type=MESH,
        )
        copy.start()
        return copy

    def add(target, sources):
        value = target[...].astype(jnp.float32)
        for source in sources:
            value = value + source[...].astype(jnp.float32)
        target[...] = value.astype(jnp.bfloat16)

    first, local = [], []
    for k in range(CHUNKS):
        columns = pl.ds(k * width, width)
        first.append(
            remote(p_ref.at[:, :, 1 - core, :, :, columns], from_core.at[k], k, 0, sibling)
        )
        copy = pltpu.make_async_copy(
            p_ref.at[:, :, core, :, :, columns], held.at[k], load_sem.at[k]
        )
        copy.start()
        local.append(copy)

    def send_e(k, x_first):
        out = []
        for d in range(1, E):
            if x_first:
                src = held.at[k, :, x, e_next[d - 1]]
                dst = from_e.at[k, d - 1, :, 0]
            else:
                src = held.at[k, :, :, e_next[d - 1]]
                dst = from_e.at[k, d - 1]
            out.append(remote(src, dst, k, d, e_peer[d - 1]))
        return out

    def send_x(k, x_first):
        if x_first:
            return [remote(held.at[k, :, 1 - x], from_x.at[k], k, E, x_peer)]
        return [remote(held.at[k, :, 1 - x, e], from_x.at[k, :, 0], k, E, x_peer)]

    def add_e(k, x_first):
        @pl.loop(0, Z)
        def _(i):
            if x_first:
                add(held.at[k, i, x, e], [from_e.at[k, d, i, 0] for d in range(E - 1)])
            else:
                for j in range(2):
                    add(held.at[k, i, j, e], [from_e.at[k, d, i, j] for d in range(E - 1)])

    def add_x(k, x_first):
        @pl.loop(0, Z)
        def _(i):
            if x_first:

                @pl.loop(0, E)
                def _(j):
                    add(held.at[k, i, x, j], [from_x.at[k, i, j]])

            else:
                add(held.at[k, i, x, e], [from_x.at[k, i, 0]])

    flying = []
    sent = []
    for k in range(CHUNKS):
        local[k].wait()
        first[k].wait_recv()

        @pl.loop(0, Z)
        def _(i):
            @pl.loop(0, E)
            def _(j):
                for m in range(2):
                    add(held.at[k, i, m, j], [from_core.at[k, i, m, j]])

        flying.append(send_x(k, True) if k % 2 else send_e(k, False))
    sent += first
    for k in range(CHUNKS):
        for copy in flying[k]:
            copy.wait_recv()
        sent += flying[k]
        if k % 2:
            add_x(k, True)
            flying[k] = send_e(k, True)
        else:
            add_e(k, False)
            flying[k] = send_x(k, False)
    for k in range(CHUNKS):
        for copy in flying[k]:
            copy.wait_recv()
        sent += flying[k]
        if k % 2:
            add_e(k, True)
        else:
            add_x(k, False)
        flying[k] = [
            remote(held.at[k, z_next[d - 1], x, e], from_z.at[k, d - 1], k, E + d, z_peer[d - 1])
            for d in range(1, Z)
        ]
    for k in range(CHUNKS):
        for copy in flying[k]:
            copy.wait_recv()
        sent += flying[k]
        value = held[k, z, x, e].astype(jnp.float32)
        for d in range(Z - 1):
            value = value + from_z[k, d].astype(jnp.float32)
        o_ref[:, k * width : (k + 1) * width] = value
    for copy in sent:
        copy.wait_send()


def reduce_over_devices(partial, count_ctx, expert_count, tok_dev):
    Z = count_ctx // 4
    E = expert_count
    width = MODEL_WIDTH // CHUNKS
    slots = E + Z
    return pl.pallas_call(
        functools.partial(reduce_kernel, Z, E),
        in_specs=[pl.BlockSpec(memory_space=pl.ANY)],
        out_specs=pl.BlockSpec(memory_space=pltpu.VMEM),
        out_shape=jax.ShapeDtypeStruct((tok_dev, MODEL_WIDTH), jnp.float32),
        scratch_shapes=[
            pltpu.VMEM((CHUNKS, Z, 2, E, tok_dev, width), jnp.bfloat16),
            pltpu.VMEM((CHUNKS, Z, 2, E, tok_dev, width), jnp.bfloat16),
            pltpu.VMEM((CHUNKS, E - 1, Z, 2, tok_dev, width), jnp.bfloat16),
            pltpu.VMEM((CHUNKS, Z, E, tok_dev, width), jnp.bfloat16),
            pltpu.VMEM((CHUNKS, Z - 1, tok_dev, width), jnp.bfloat16),
            pltpu.SemaphoreType.DMA((CHUNKS,)),
            pltpu.SemaphoreType.DMA((CHUNKS, slots)),
            pltpu.SemaphoreType.DMA((CHUNKS, slots)),
        ],
        compiler_params=pltpu.CompilerParams(
            collective_id=0, has_side_effects=True, vmem_limit_bytes=VMEM_LIMIT
        ),
        name="reduce_over_devices",
    )(partial.reshape(Z, 2, 2, E, tok_dev, MODEL_WIDTH))


VMEM_LIMIT = 60 * 1024 * 1024


def shards(
    hidden,
    lengths,
    routes,
    gates,
    attn_gain,
    q_weight,
    key_value_weight,
    q_gain,
    k_gain,
    o_weight,
    moe_gain,
    expert_in,
    expert_out,
):
    count_ctx = lax.axis_size("ctx")
    expert_count = lax.axis_size("exp")
    my_ctx = lax.axis_index("ctx")
    my_exp = lax.axis_index("exp")
    tok_dev = hidden.shape[0]
    tok_ctx = tok_dev * expert_count
    half_rows = tok_ctx // 2
    head_groups = QUERY_HEADS // KEY_VALUE_HEADS
    q_dev = QUERY_HEADS // expert_count
    key_value_share = max(1, KEY_VALUE_HEADS // expert_count)
    group_dev = q_dev // key_value_share
    column_share = KEY_VALUE_HEADS * HEAD_SIZE // expert_count
    key_value_leading = my_exp * q_dev // head_groups
    col_offset = my_exp * column_share - key_value_leading * HEAD_SIZE
    query_pos = mirrored_position(
        my_ctx * tok_ctx + jnp.arange(tok_ctx, dtype=jnp.int32), count_ctx, tok_ctx
    )
    query_doc, query_rope = document_info(query_pos, lengths)
    normed_own = rms_scale(hidden.astype(jnp.float32), attn_gain).astype(jnp.bfloat16)
    pieces = [normed_own]
    for shift in range(1, expert_count):
        route = [(i, (i + shift) % expert_count) for i in range(expert_count)]
        pieces.append(lax.ppermute(normed_own, "exp", route))
    stacked = jnp.stack(pieces)
    normed = jnp.concatenate(
        [
            lax.dynamic_index_in_dim(stacked, (my_exp - j) % expert_count, 0, keepdims=False)
            for j in range(expert_count)
        ],
        axis=0,
    )
    key_cols = lax.dynamic_slice_in_dim(
        key_value_weight, key_value_leading * HEAD_SIZE, key_value_share * HEAD_SIZE, 1
    )
    value_column_block = lax.dynamic_slice_in_dim(
        key_value_weight,
        KEY_VALUE_HEADS * HEAD_SIZE + key_value_leading * HEAD_SIZE,
        key_value_share * HEAD_SIZE,
        1,
    )
    kv_local = jnp.concatenate([key_cols, value_column_block], axis=1)
    weights = lax.all_gather(
        jnp.concatenate([q_weight, kv_local, o_weight.T], axis=1), "ctx", axis=0, tiled=True
    )
    q_width = q_weight.shape[1]
    kv_width = kv_local.shape[1]
    projected = jnp.dot(
        normed, weights[:, : q_width + kv_width], preferred_element_type=jnp.float32
    )
    q_raw = projected[:, :q_width]
    key_value_plain = projected[:, q_width:]
    queries = rotate(
        rms_scale(q_raw.reshape(tok_ctx, q_dev, HEAD_SIZE), q_gain), query_rope
    ).astype(jnp.bfloat16)
    key_row_block = rotate(
        rms_scale(
            key_value_plain[:, : key_value_share * HEAD_SIZE].reshape(
                tok_ctx, key_value_share, HEAD_SIZE
            ),
            k_gain,
        ),
        query_rope,
    ).astype(jnp.bfloat16)
    value_row_block = key_value_plain[:, key_value_share * HEAD_SIZE :].astype(jnp.bfloat16)
    key_values = jnp.stack(
        [key_row_block.reshape(tok_ctx, key_value_share * HEAD_SIZE), value_row_block]
    )
    gathered = lax.all_gather(key_values, "ctx", axis=0)
    ordered = jnp.concatenate(
        [
            jnp.moveaxis(gathered[:, :, :half_rows], 0, 1),
            jnp.moveaxis(gathered[::-1, :, half_rows:], 0, 1),
        ],
        axis=1,
    ).reshape(2, count_ctx * tok_ctx, key_value_share * HEAD_SIZE)
    cache = lax.dynamic_slice(
        ordered, (0, my_ctx * tok_ctx, col_offset), (2, tok_ctx, column_share)
    )
    context = attention(
        lengths,
        queries.reshape(tok_ctx, q_dev * HEAD_SIZE),
        ordered[0],
        ordered[1],
        count_ctx,
        half_rows,
        key_value_share,
        group_dev,
    )
    o_rows = weights[:, q_width + kv_width :]
    attn_part = lax.dot_general(
        context, o_rows, (((1,), (1,)), ((), ())), preferred_element_type=jnp.float32
    )
    attn_parts = attn_part.reshape(expert_count, tok_dev, MODEL_WIDTH)
    attn_own = lax.dynamic_index_in_dim(attn_parts, my_exp, 0, keepdims=False)
    for shift in range(1, expert_count):
        outgoing = lax.dynamic_index_in_dim(
            attn_parts, (my_exp + shift) % expert_count, 0, keepdims=False
        ).astype(jnp.bfloat16)
        route = [(i, (i + shift) % expert_count) for i in range(expert_count)]
        attn_own = attn_own + lax.ppermute(outgoing, "exp", route).astype(jnp.float32)
    residual_mid = hidden.astype(jnp.float32) + attn_own
    moe_in = rms_scale(residual_mid, moe_gain).astype(jnp.bfloat16)
    devices = count_ctx * expert_count
    slices = max(1, devices // EXPERTS)
    rows_dev = expert_in.shape[0]
    ffs_dev = expert_out.shape[1]
    capacity = max(4, 2 * tok_dev * TOP // EXPERTS)
    tokens = lax.all_gather(moe_in, ("ctx", "exp"), axis=0)
    table = lax.all_gather(
        jnp.concatenate([routes.astype(jnp.float32), gates], axis=1), ("ctx", "exp"), axis=0
    )
    my_device = my_ctx * expert_count + my_exp
    my_experts = (my_device * rows_dev + jnp.arange(rows_dev, dtype=jnp.int32)) // slices
    chosen = (
        table[:, None, :, :TOP].astype(jnp.int32) == my_experts[None, :, None, None]
    )
    hit = jnp.any(chosen, axis=3)
    token_gate = jnp.sum(jnp.where(chosen, table[:, None, :, TOP:], 0.0), axis=3)
    before = jnp.triu(jnp.ones((tok_dev, tok_dev), jnp.bfloat16), 1)
    ranking = jnp.einsum(
        "ait,tu->aiu", hit.astype(jnp.bfloat16), before, preferred_element_type=jnp.float32
    ).astype(jnp.int32)
    placed = hit[:, :, None, :] & (
        ranking[:, :, None, :] == jnp.arange(capacity, dtype=jnp.int32)[None, None, :, None]
    )
    slot_gate = jnp.sum(jnp.where(placed, token_gate[:, :, None, :], 0.0), axis=3)
    placement = placed.astype(jnp.bfloat16).reshape(devices, rows_dev * capacity, tok_dev)
    arrived = (
        jnp.einsum("ast,atd->asd", placement, tokens, preferred_element_type=jnp.float32)
        .astype(jnp.bfloat16)
        .reshape(devices, rows_dev, capacity, MODEL_WIDTH)
    )
    gate_up = jnp.einsum("arcd,rdf->arcf", arrived, expert_in, preferred_element_type=jnp.float32)
    activated = (
        jax.nn.silu(gate_up[..., :ffs_dev]) * gate_up[..., ffs_dev:] * slot_gate[..., None]
    ).astype(jnp.bfloat16)
    produced = jnp.einsum(
        "arcf,rfd->arcd", activated, expert_out, preferred_element_type=jnp.float32
    ).astype(jnp.bfloat16)
    partial = jnp.einsum(
        "ast,asd->atd",
        placement,
        produced.reshape(devices, rows_dev * capacity, MODEL_WIDTH),
        preferred_element_type=jnp.float32,
    ).astype(jnp.bfloat16)
    moe_out = reduce_over_devices(partial, count_ctx, expert_count, tok_dev)
    new_hidden = (residual_mid + moe_out).astype(jnp.bfloat16)
    return (new_hidden, cache)


def solution(mesh):
    in_specs = (
        P(("ctx", "exp"), None),
        P(),
        P(("ctx", "exp"), None),
        P(("ctx", "exp"), None),
        P(),
        P("ctx", "exp"),
        P("ctx", None),
        P(),
        P(),
        P("exp", "ctx"),
        P(),
        P(("ctx", "exp"), None, None),
        P(("ctx", "exp"), None, None),
    )
    out_specs = (P(("ctx", "exp"), None), P(None, "ctx", "exp"))
    return jax.shard_map(shards, mesh=mesh, in_specs=in_specs, out_specs=out_specs, check_vma=False)
```
